512 devices in a mesh: section: 32 (over x, y), expert: 16 (over z, core).
Axes of the slice: x: 4, y: 8, z: 8, core: 2. Of those that a mesh axis runs over, the one named last changes fastest.
Arguments:
- tokens: bfloat16 [32, 2048, 1024], P('section', 'expert'), may hold values from -6 to 6
- routes: int32 [32, 2048, 8], P('section'), may hold values from 0 to 15, all different within a row
- route_weight: float32 [32, 2048, 8], P('section'), may hold values from 0.1 to 1
- projections: bfloat16 [32, 16, 3, 1024, 384], P('section', 'expert'), may hold values from -0.91855865 to 0.91855865
Outputs:
- merged: bfloat16 [32, 16, 3, 1024, 192], P('section', 'expert')
- handed: bfloat16 [32, 2048, 1024], P('section', 'expert')
The draws below stay inside these ranges and needn't reach their ends.
Inputs may be any that keep to these rules, and one draw needn't show every extreme that they name: `routes`: each token names 8 different experts of 0 to 15, and every one of them is named by some token of each layer.
All inputs are finite; a program needn't handle non-finite values.
Results may differ from the reference program's by a relative error of at most 0.02.
Values may be sent and summed in bfloat16 or wider, within the bound.
No kernel may reach another device: no remote copies, remote signals or barrier semaphores. Data moves between devices by JAX's collectives and lax.ppermute only.
A program may use at most 64 MiB of HBM per device.

```python
import jax
import jax.numpy as jnp
from jax import lax

D = 1024
FF = 384
LAYERS = 32
EXPERTS = 16
TOP = 8
TOKENS = 2048


def draw_projections(key, part):
    key = jax.random.fold_in(key, 7)
    subkeys = jax.random.split(key, 5)
    pair_count = EXPERTS // 2
    full_shape = (LAYERS, pair_count, 3, D, FF)
    unit_shape = (LAYERS, pair_count, 3, 1, FF)
    shared = jnp.clip(jax.random.normal(subkeys[0], full_shape, jnp.float32), -4.0, 4.0)
    independent = jnp.clip(jax.random.normal(subkeys[1], full_shape, jnp.float32), -4.0, 4.0)
    mixing = jax.random.uniform(subkeys[2], unit_shape, jnp.float32, 0.0, 0.95)
    scale_low = jnp.exp(jax.random.uniform(subkeys[3], unit_shape, jnp.float32, -1.15, 1.15))
    scale_high = jnp.exp(jax.random.uniform(subkeys[4], unit_shape, jnp.float32, -1.15, 1.15))
    fan_scale = jnp.array([D ** (-0.5), D ** (-0.5), FF ** (-0.5)], jnp.float32).reshape(1, 1, 3, 1, 1)
    low_side = shared * scale_low * fan_scale
    high_side = (mixing * shared + jnp.sqrt(1.0 - mixing * mixing) * independent) * scale_high * fan_scale
    return jnp.concatenate([low_side, high_side], axis=1).astype(jnp.bfloat16)


def level_of(stream_key, dims, shards, smallest, high):
    level, own = 1.0, jax.random.fold_in(stream_key, 6)
    for dim, blocks in shards:
        heights = jnp.exp(jax.random.uniform(jax.random.fold_in(own, dim), (blocks,), jnp.float32, smallest / len(shards), high / len(shards)))
        level = level * jnp.repeat(heights, dims[dim] // blocks).reshape([-1 if axis == dim else 1 for axis in range(len(dims))])
    return level


def picks_of(own_key, rows, number_of, top, lift):
    order = jax.random.permutation(jax.random.fold_in(own_key, 1), number_of)
    boost = order
    for power in range(3):
        boost = boost * boost // number_of
    boost = boost * lift // number_of
    lots = jax.random.randint(jax.random.fold_in(own_key, 2), (rows, number_of), 0, 4096) + boost
    fixed_rows = jax.random.permutation(jax.random.fold_in(own_key, 3), rows)[jnp.arange(number_of) % rows]
    lots = jnp.where(jnp.arange(rows)[:, None] == fixed_rows[None, :], 1 << 14, lots)
    priority = lots * number_of + jnp.arange(number_of)
    return lax.top_k(priority.astype(jnp.int32), top)[1].astype(jnp.int32)


def noise(rng, dims, scale, reach, cuts=(), kind=jnp.bfloat16):
    loudness = level_of(rng, dims, cuts, -0.22, 0.18) if cuts else 1.0
    values = jax.random.normal(rng, dims, jnp.float32) * scale * loudness
    return jnp.minimum(jnp.maximum(values, -reach), reach).astype(kind)


def setup_inputs(seed: int = 0) -> dict:
    key_of = jax.random.split(jax.random.key(seed), 5)
    return {
        "tokens": noise(key_of[0], (LAYERS, TOKENS, D), 1.0, 6.0, ((0, 32), (1, 16))),
        "routes": picks_of(key_of[1], LAYERS * TOKENS, EXPERTS, TOP, 4096).reshape((LAYERS, TOKENS, TOP)),
        "route_weight": jnp.clip(0.1 + 0.9 * jax.random.uniform(key_of[2], (LAYERS, TOKENS, TOP), jnp.float32) ** level_of(key_of[2], (LAYERS, TOKENS, TOP), ((0, 32),), -0.2, 0.2), 0.1, 1.0),
        "projections": draw_projections(jax.random.fold_in(key_of[4], 71), 0),
    }


EPS = 1e-06

def silu_mix(activations, gate_matrix, up_matrix):
    gate_out = jnp.dot(activations, gate_matrix, preferred_element_type=jnp.float32)
    up_out = jnp.dot(activations, up_matrix, preferred_element_type=jnp.float32)
    return (jax.nn.silu(gate_out) * up_out).astype(jnp.bfloat16)

def one_layer(layer_args):
    layer_tokens, layer_routes, layer_weight, layer_proj = layer_args
    pair_count = EXPERTS // 2
    half_units = FF // 2
    hidden = lax.map(lambda stack: silu_mix(layer_tokens, stack[0], stack[1]), layer_proj)
    expert_ids = jnp.arange(EXPERTS, dtype=jnp.int32)
    matches = layer_routes[:, :, None] == expert_ids[None, None, :]
    member_all = lax.optimization_barrier(jnp.sum(matches.astype(jnp.float32), axis=1))
    weight_all = lax.optimization_barrier(jnp.sum(jnp.where(matches, layer_weight[:, :, None], jnp.float32(0.0)), axis=1))
    members = member_all[:, :pair_count] + member_all[:, pair_count:]
    pair_weight = weight_all[:, :pair_count] + weight_all[:, pair_count:]
    used_rows = jnp.maximum(lax.optimization_barrier(jnp.sum(members, axis=0)), jnp.float32(1.0))
    low_hidden = hidden[:pair_count].astype(jnp.float32)
    high_hidden = hidden[pair_count:].astype(jnp.float32)
    selector = jnp.transpose(members)[:, :, None]
    energy_low = lax.optimization_barrier(jnp.sum(selector * low_hidden * low_hidden, axis=1)) / used_rows[:, None]
    energy_high = lax.optimization_barrier(jnp.sum(selector * high_hidden * high_hidden, axis=1)) / used_rows[:, None]
    cross_term = lax.optimization_barrier(jnp.sum(selector * low_hidden * high_hidden, axis=1)) / used_rows[:, None]
    agreement = 0.5 * (1.0 + cross_term / jnp.sqrt(energy_low * energy_high + EPS))
    root_low = jnp.sqrt(energy_low + EPS)
    root_high = jnp.sqrt(energy_high + EPS)
    blend = root_low / (root_low + agreement * root_high)
    blend_wide = blend[:, None, None, :]
    low_proj = layer_proj[:pair_count].astype(jnp.float32)
    high_proj = layer_proj[pair_count:].astype(jnp.float32)
    merged_full = (blend_wide * low_proj + (1.0 - blend_wide) * high_proj).astype(jnp.bfloat16)
    merged = jnp.concatenate([merged_full[..., :half_units], merged_full[..., half_units:]], axis=0)
    row_weights = jnp.transpose(jnp.concatenate([pair_weight, pair_weight], axis=1))

    def add_expert(running, scan_in):
        expert_merged, expert_weight = scan_in
        inner = silu_mix(layer_tokens, expert_merged[0], expert_merged[1])
        product = jnp.dot(inner, jnp.transpose(expert_merged[2]), preferred_element_type=jnp.float32)
        partial_term = (expert_weight[:, None] * product).astype(jnp.bfloat16)
        partial_term = lax.optimization_barrier(partial_term)
        return (running + partial_term.astype(jnp.float32), None)
    total, _ = lax.scan(add_expert, jnp.zeros((TOKENS, D), jnp.float32), (merged, row_weights))
    block_out = (layer_tokens.astype(jnp.float32) + total).astype(jnp.bfloat16)
    return (merged, block_out)

def reference(tokens, routes, route_weight, projections):
    merged, blocks = lax.map(one_layer, (tokens, routes, route_weight, projections))
    handed = jnp.concatenate([jnp.zeros((1, TOKENS, D), jnp.bfloat16), blocks[:-1]], axis=0)
    return (merged, handed)
```

```python
import jax
import jax.numpy as jnp
from jax import lax
from jax.sharding import PartitionSpec as P

EPS = 1e-06
CORES = 2


def along(array, count, target):
    return lax.ppermute(array, "expert", [(i, target(i)) for i in range(count)])


def ring(count, steps):
    return lambda i: (i + CORES * steps) % count


def next_layer(array, target):
    layers, count = lax.axis_size("section"), lax.axis_size("expert")
    route = [
        (layer * count + i, (layer + 1) * count + target(i))
        for layer in range(layers - 1)
        for i in range(count)
    ]
    return lax.ppermute(array, ("section", "expert"), route)


def against(activations, matrix):
    return lax.dot_general(
        activations, matrix, (((1,), (1,)), ((), ())), preferred_element_type=jnp.float32
    )


def silu_mix(activations, gate_matrix, up_matrix):
    return jax.nn.silu(against(activations, gate_matrix)) * against(activations, up_matrix)


def local(tokens, routes, route_weight, projections):
    x_local = tokens[0]
    layer_routes = routes[0]
    layer_weight = route_weight[0]
    weights = jnp.swapaxes(projections[0, 0], 1, 2)
    count = lax.axis_size("expert")
    pair_count = count // 2
    chips = count // CORES
    me = lax.axis_index("expert")
    chip, core = me // CORES, me % CORES
    is_upper = me >= pair_count
    half_units = weights.shape[1] // 2
    own_start = jnp.where(is_upper, half_units, 0).astype(jnp.int32)
    other_start = half_units - own_start
    rows = x_local.shape[0]

    mine_w = lax.dynamic_slice_in_dim(weights, own_start, half_units, 1)
    send_w = lax.dynamic_slice_in_dim(weights, other_start, half_units, 1)
    across = lambda i: (i + pair_count) % count
    partner_in = along(send_w[:2], count, across)
    send_down, partner_in = lax.optimization_barrier((send_w[2], partner_in))
    partner_down = along(send_down, count, across)
    x_all = lax.all_gather(x_local, "expert", axis=0, tiled=True)

    lower_id = me % pair_count

    def routed(pair):
        return (layer_routes == pair) | (layer_routes == pair + pair_count)

    def weight_of(pair):
        return jnp.sum(jnp.where(routed(pair), layer_weight, jnp.float32(0.0)), axis=1)

    members = jnp.sum(routed(lower_id).astype(jnp.float32), axis=1)
    used_rows = jnp.maximum(jnp.sum(members), jnp.float32(1.0))

    mine_f = silu_mix(x_all, mine_w[0], mine_w[1]).astype(jnp.bfloat16).astype(jnp.float32)
    partner_f = silu_mix(x_all, partner_in[0], partner_in[1]).astype(jnp.bfloat16).astype(jnp.float32)
    selector = members[:, None]
    energy_mine = jnp.sum(selector * mine_f * mine_f, axis=0) / used_rows
    energy_partner = jnp.sum(selector * partner_f * partner_f, axis=0) / used_rows
    cross_term = jnp.sum(selector * mine_f * partner_f, axis=0) / used_rows
    energy_low = jnp.where(is_upper, energy_partner, energy_mine)
    energy_high = jnp.where(is_upper, energy_mine, energy_partner)
    agreement = 0.5 * (1.0 + cross_term / jnp.sqrt(energy_low * energy_high + EPS))
    root_low = jnp.sqrt(energy_low + EPS)
    root_high = jnp.sqrt(energy_high + EPS)
    blend = root_low / (root_low + agreement * root_high)
    of_mine = jnp.where(is_upper, 1.0 - blend, blend)[:, None]
    of_partner = jnp.where(is_upper, blend, 1.0 - blend)[:, None]

    def merge(own, other):
        return (of_mine * own.astype(jnp.float32) + of_partner * other.astype(jnp.float32)).astype(jnp.bfloat16)

    sibling = lambda i: i ^ 1
    merged_in = merge(mine_w[:2], partner_in)
    sibling_in = along(merged_in, count, sibling)
    merged_down = merge(mine_w[2], partner_down)
    sibling_down = along(merged_down, count, sibling)

    def of_core(array):
        blocks = array.reshape(chips, CORES, rows, *array.shape[1:])
        blocks = lax.dynamic_index_in_dim(blocks, core, 1, keepdims=False)
        blocks = jnp.concatenate([blocks, blocks], axis=0)
        return lax.dynamic_slice_in_dim(blocks, chip, chips, 0).reshape(chips * rows, *array.shape[1:])

    x_core = of_core(x_all)
    own_weight = of_core(weight_of(lower_id))[:, None]
    sibling_weight = of_core(weight_of(lower_id ^ 1))[:, None]
    inner = jnp.concatenate(
        [
            (own_weight * silu_mix(x_core, merged_in[0], merged_in[1])).astype(jnp.bfloat16),
            (sibling_weight * silu_mix(x_core, sibling_in[0], sibling_in[1])).astype(jnp.bfloat16),
        ],
        axis=1,
    )
    down = jnp.concatenate([merged_down, sibling_down], axis=0)
    terms = jnp.dot(inner, down, preferred_element_type=jnp.float32).astype(jnp.bfloat16)
    terms = terms.reshape(chips, rows, -1)
    half = rows // 2
    far = chips // 2

    def add(a, b):
        return (a.astype(jnp.float32) + b.astype(jnp.float32)).astype(jnp.bfloat16)

    def collect(sign, first, second):
        at = lambda steps: terms[(sign * steps) % chips]
        far_rows = along(at(far)[first:second], count, ring(count, 2 * sign))
        near = along(at(far - 1), count, ring(count, sign))
        own = at(far - 2).astype(jnp.float32) + near.astype(jnp.float32)
        patch = own[first:second] + far_rows.astype(jnp.float32)
        parts = [patch, own[half:]] if first == 0 else [own[:half], patch]
        partial = jnp.concatenate(parts, axis=0).astype(jnp.bfloat16)
        for steps in range(far - 3, 0, -1):
            partial = add(along(partial, count, ring(count, sign)), at(steps))
        return next_layer(partial, ring(count, sign))

    onward = collect(1, 0, half)
    backward = collect(-1, half, rows)
    kept = next_layer(add(x_local, terms[0]), lambda i: i)
    handed = (kept.astype(jnp.float32) + onward.astype(jnp.float32) + backward.astype(jnp.float32)).astype(jnp.bfloat16)
    merged = jnp.concatenate([merged_in, merged_down[None]], axis=0)
    return (jnp.swapaxes(merged, 1, 2)[None, None], handed[None])


def solution(mesh):
    in_specs = (
        P("section", "expert", None),
        P("section", None, None),
        P("section", None, None),
        P("section", "expert", None, None, None),
    )
    out_specs = (P("section", "expert", None, None, None), P("section", "expert", None))
    return jax.shard_map(local, mesh=mesh, in_specs=in_specs, out_specs=out_specs, check_vma=False)
```

```python
import jax
import jax.numpy as jnp
from jax import lax
from jax.experimental import pallas as pl
from jax.experimental.pallas import tpu as pltpu
from jax.sharding import PartitionSpec as P

EPS = 1e-06
CORES = 2
SLAB = 256


def along(array, count, target):
    return lax.ppermute(array, "expert", [(i, target(i)) for i in range(count)])


def ring(count, steps):
    return lambda i: (i + CORES * steps) % count


def next_layer(array, target):
    layers, count = lax.axis_size("section"), lax.axis_size("expert")
    route = [
        (layer * count + i, (layer + 1) * count + target(i))
        for layer in range(layers - 1)
        for i in range(count)
    ]
    return lax.ppermute(array, ("section", "expert"), route)


def against(matrix, activations):
    return lax.dot_general(
        matrix, activations, (((1,), (1,)), ((), ())), preferred_element_type=jnp.float32
    )


def silu_mix(gate, up):
    return gate / (1.0 + jnp.exp(-gate)) * up


def merge(is_upper, blend, own, other):
    of_own = jnp.where(is_upper, 1.0 - blend, blend)
    of_other = jnp.where(is_upper, blend, 1.0 - blend)
    return (of_own * own.astype(jnp.float32) + of_other * other.astype(jnp.float32)).astype(jnp.bfloat16)


def split_kernel(upper, projection, kept_in, kept_down, sent_in, sent_down):
    units = kept_down.shape[0]
    part = pl.program_id(0)
    turned = projection[0].T

    def put(kept, sent, at):
        @pl.when(upper[0] == 1)
        def _():
            kept[at, :] = turned[units:]
            sent[at, :] = turned[:units]

        @pl.when(upper[0] == 0)
        def _():
            kept[at, :] = turned[:units]
            sent[at, :] = turned[units:]

    for matrix in range(2):

        @pl.when(part == matrix)
        def _(matrix=matrix):
            put(kept_in, sent_in, pl.ds(matrix * units, units))

    @pl.when(part == 2)
    def _():
        put(kept_down, sent_down, pl.ds(0, units))


def blend_kernel(upper, members, x, own, other, merged, blend_out, sums, count):
    step = pl.program_id(0)
    units = sums.shape[1]
    lanes = sums.shape[2]

    @pl.when(step == 0)
    def _():
        sums[...] = jnp.zeros_like(sums)
        count[...] = jnp.zeros_like(count)

    def fold(array):
        return sum(array[:, i : i + lanes] for i in range(0, array.shape[1], lanes))

    for start in range(0, x.shape[0], SLAB):
        slab = pl.ds(start, SLAB)
        chosen = members[0][:, start : start + SLAB]
        hidden = []
        for weights in (own, other):
            out = against(weights[...], x[slab, :])
            hidden.append(silu_mix(out[:units], out[units:]).astype(jnp.bfloat16).astype(jnp.float32))
        mine, theirs = hidden
        weighted = chosen * mine
        sums[0] += fold(weighted * mine)
        sums[1] += fold(chosen * theirs * theirs)
        sums[2] += fold(weighted * theirs)
        count[...] += fold(chosen)

    @pl.when(step == pl.num_programs(0) - 1)
    def _():
        is_upper = upper[0] == 1
        used = jnp.maximum(jnp.sum(count[...], axis=1, keepdims=True), 1.0)
        energy_own, energy_other, cross_term = (
            jnp.sum(sums[i], axis=1, keepdims=True) / used for i in range(3)
        )
        energy_low = jnp.where(is_upper, energy_other, energy_own)
        energy_high = jnp.where(is_upper, energy_own, energy_other)
        agreement = 0.5 * (1.0 + cross_term / jnp.sqrt(energy_low * energy_high + EPS))
        root_low = jnp.sqrt(energy_low + EPS)
        root_high = jnp.sqrt(energy_high + EPS)
        blend = root_low / (root_low + agreement * root_high)
        blend_out[...] = jnp.broadcast_to(blend, blend_out.shape)
        for part in range(2):
            at = pl.ds(part * units, units)
            merged[at, :] = merge(is_upper, blend, own[at, :], other[at, :])


def weighted_terms(gate, up, down, x, weights, outs):
    units = gate.shape[0] // 2
    hidden = jnp.concatenate([ref[...] for ref in x], axis=0)
    hidden = silu_mix(against(gate[...], hidden), against(up[...], hidden))
    weight = jnp.concatenate([ref[0] for ref in weights], axis=1)
    inner = jnp.concatenate([hidden[:units] * weight[:1], hidden[units:] * weight[1:]], axis=0)
    out = lax.dot_general(
        inner.astype(jnp.bfloat16), down[...], (((0,), (0,)), ((), ())), preferred_element_type=jnp.float32
    ).astype(jnp.bfloat16)
    start = 0
    for ref in outs:
        ref[...] = out[start : start + ref.shape[0]]
        start += ref.shape[0]


def first_kernel(
    places, upper, weight_a, weight_b, weight_c, weight_d, x_a, x_b, x_c, x_d, merged_in, own_down, other_down,
    next_own, next_other, next_own_down, next_down, blend, next_blend, term_a, term_b, term_c, term_d, term_e, gate, up, down
):
    units = blend.shape[0]
    is_upper = upper[0] == 1
    mine = blend[:, :1]
    theirs = next_blend[:, :1]
    gate[:units] = merged_in[:units]
    up[:units] = merged_in[units:]
    down[:units] = merge(is_upper, mine, own_down[...], other_down[...])
    gate[units:] = merge(is_upper, theirs, next_own[:units], next_other[:units])
    up[units:] = merge(is_upper, theirs, next_own[units:], next_other[units:])
    down[units:] = merge(is_upper, theirs, next_own_down[...], next_down[...])
    weighted_terms(gate, up, down, (x_a, x_b), (weight_a, weight_b), (term_a, term_b, term_c))
    weighted_terms(gate, up, down, (x_c, x_d), (weight_c, weight_d), (term_d, term_e))


def terms_kernel(places, weight_a, weight_b, x_a, x_b, gate, up, down, *outs):
    for step in range(len(outs) // 2):

        @pl.when(pl.program_id(0) == step)
        def _(step=step):
            weighted_terms(gate, up, down, (x_a, x_b), (weight_a, weight_b), outs[2 * step : 2 * step + 2])


def local(tokens, routes, route_weight, projections):
    x_local = tokens[0]
    layer_routes = routes[0]
    layer_weight = route_weight[0]
    count = lax.axis_size("expert")
    pair_count = count // 2
    chips = count // CORES
    me = lax.axis_index("expert")
    chip, core = me // CORES, me % CORES
    is_upper = me >= pair_count
    upper = is_upper.astype(jnp.int32)[None]
    matrices, features, full_units = projections.shape[2:]
    units = full_units // 2
    rows = x_local.shape[0]
    across = lambda i: (i + pair_count) % count
    sibling = lambda i: i ^ 1

    x_all = lax.all_gather(x_local, "expert", axis=0, tiled=True)
    half_spec = lambda parts: pl.BlockSpec((parts * units, features), lambda i, *_: (0, 0))
    half = lambda parts: jax.ShapeDtypeStruct((parts * units, features), jnp.bfloat16)
    mine_in, mine_down, send_in, send_down = pl.pallas_call(
        split_kernel,
        grid_spec=pltpu.PrefetchScalarGridSpec(
            num_scalar_prefetch=1,
            grid=(matrices,),
            in_specs=[pl.BlockSpec((1, features, full_units), lambda i, *_: (i, 0, 0))],
            out_specs=[half_spec(2), half_spec(1), half_spec(2), half_spec(1)],
        ),
        out_shape=[half(2), half(1), half(2), half(1)],
        compiler_params=pltpu.CompilerParams(vmem_limit_bytes=32 << 20),
        cost_estimate=pl.CostEstimate(flops=0, bytes_accessed=4 * matrices * features * full_units, transcendentals=0),
        name="split",
    )(upper, projections[0, 0])
    partner_in = along(send_in, count, across)
    send_down, partner_in = lax.optimization_barrier((send_down, partner_in))
    partner_down = along(send_down, count, across)
    next_other = along(partner_in, count, sibling)

    members, row_weight = [], []
    for pair in (me % pair_count, (me % pair_count) ^ 1):
        named = (layer_routes == pair) | (layer_routes == pair + pair_count)
        members.append(jnp.sum(named.astype(jnp.float32), axis=1))
        row_weight.append(jnp.sum(jnp.where(named, layer_weight, jnp.float32(0.0)), axis=1))
    row_weight = jnp.stack([array.reshape(count, rows) for array in row_weight], axis=1)
    far = chips // 2
    order = [far, far - 1, far + 1, 0, *(s for k in range(far - 2, 0, -1) for s in (k, chips - k))]
    places = ((chip + jnp.array(order, jnp.int32)) % chips) * CORES + core
    member, row_weight, first_places, places, kept_in, kept_down = lax.optimization_barrier(
        (members[0].reshape(-1, 1, 4 * rows), row_weight, places[:4], places[4:], mine_in, mine_down)
    )
    next_own = along(kept_in, count, sibling)
    next_own_down = along(kept_down, count, sibling)

    whole = lambda shape: pl.BlockSpec(shape, lambda i, *_: (0,) * len(shape))
    held = pl.BlockSpec(memory_space=pltpu.VMEM)
    total = x_all.shape[0]
    group = 4 * rows
    merged_in, blend = pl.pallas_call(
        blend_kernel,
        grid_spec=pltpu.PrefetchScalarGridSpec(
            num_scalar_prefetch=1,
            grid=(total // group,),
            in_specs=[
                pl.BlockSpec((1, 1, group), lambda i, *_: (i, 0, 0)),
                pl.BlockSpec((group, features), lambda i, *_: (i, 0)),
                held,
                held,
            ],
            out_specs=[whole((2 * units, features)), whole((units, 128))],
            scratch_shapes=[pltpu.VMEM((3, units, 128), jnp.float32), pltpu.VMEM((1, 128), jnp.float32)],
        ),
        out_shape=[
            jax.ShapeDtypeStruct((2 * units, features), jnp.bfloat16),
            jax.ShapeDtypeStruct((units, 128), jnp.float32),
        ],
        compiler_params=pltpu.CompilerParams(vmem_limit_bytes=32 << 20),
        cost_estimate=pl.CostEstimate(flops=8 * total * units * features, bytes_accessed=2 * total * features, transcendentals=0),
        name="blend",
    )(upper, member, x_all, mine_in, partner_in)
    next_blend = along(blend, count, sibling)
    partner_down, blend = lax.optimization_barrier((partner_down, blend))
    next_down = along(partner_down, count, sibling)

    weight_spec = lambda k: pl.BlockSpec((1, CORES, rows), lambda i, place, *_: (place[2 * i + k], 0, 0))
    x_spec = lambda k: pl.BlockSpec((rows, features), lambda i, place, *_: (place[2 * i + k], 0))
    blocks_in = lambda number: [weight_spec(k) for k in range(number)] + [x_spec(k) for k in range(number)]
    both = (2 * units, features)
    block = jax.ShapeDtypeStruct((rows, features), jnp.bfloat16)
    part = jax.ShapeDtypeStruct((rows // 2, features), jnp.bfloat16)
    low_rows, high_rows, *firsts, gate, up, down = pl.pallas_call(
        first_kernel,
        grid_spec=pltpu.PrefetchScalarGridSpec(
            num_scalar_prefetch=2,
            grid=(1,),
            in_specs=[
                *blocks_in(4),
                *[held] * 9,
            ],
            out_specs=[whole(part.shape)] * 2 + [whole(block.shape)] * 3 + [whole(both)] * 3,
        ),
        out_shape=[part] * 2 + [block] * 3 + [jax.ShapeDtypeStruct(both, jnp.bfloat16)] * 3,
        compiler_params=pltpu.CompilerParams(vmem_limit_bytes=40 << 20),
        cost_estimate=pl.CostEstimate(flops=24 * rows * units * features, bytes_accessed=20 * units * features, transcendentals=0),
        name="first",
    )(first_places, upper, *[row_weight] * 4, *[x_all] * 4, merged_in, mine_down, partner_down,
      next_own, next_other, next_own_down, next_down, blend, next_blend)
    others = pl.pallas_call(
        terms_kernel,
        grid_spec=pltpu.PrefetchScalarGridSpec(
            num_scalar_prefetch=1,
            grid=(chips // 2 - 2,),
            in_specs=[*blocks_in(2), whole(both), whole(both), whole(both)],
            out_specs=[whole(block.shape)] * (chips - 4),
        ),
        out_shape=[block] * (chips - 4),
        compiler_params=pltpu.CompilerParams(vmem_limit_bytes=40 << 20),
        cost_estimate=pl.CostEstimate(flops=24 * rows * units * features, bytes_accessed=4 * chips * rows * features, transcendentals=0),
        name="terms",
    )(places, row_weight, row_weight, x_all, x_all, gate, up, down)
    terms = dict(zip(order[1:], [*firsts, *others]))

    def add(*parts):
        return sum(part.astype(jnp.float32) for part in parts).astype(jnp.bfloat16)

    half = rows // 2
    behind, ahead = along(low_rows, count, ring(count, 1)), along(high_rows, count, ring(count, -1))
    three, minus_three = terms[far - 1], terms[chips - far + 1]
    grown = jnp.concatenate([add(behind, three[:half]), three[half:]], axis=0)
    minus_grown = jnp.concatenate([minus_three[:half], add(ahead, minus_three[half:])], axis=0)
    grown, minus_grown, one, minus_one = lax.optimization_barrier((grown, minus_grown, terms[1], terms[chips - 1]))
    grown = add(along(grown, count, ring(count, 1)), terms[far - 2])
    minus_grown = add(along(minus_grown, count, ring(count, -1)), terms[chips - far + 2])
    here = add(x_local, terms[0], along(one, count, ring(count, 1)), along(minus_one, count, ring(count, -1)))
    handed = add(
        next_layer(grown, ring(count, far - 2)),
        next_layer(minus_grown, ring(count, 2 - far)),
        next_layer(here, lambda i: i),
    )
    own = jnp.stack([gate[:units], up[:units], down[:units]])
    return (jnp.swapaxes(own, 1, 2)[None, None], handed[None])


def solution(mesh):
    in_specs = (
        P("section", "expert", None),
        P("section", None, None),
        P("section", None, None),
        P("section", "expert", None, None, None),
    )
    out_specs = (P("section", "expert", None, None, None), P("section", "expert", None))
    return jax.shard_map(local, mesh=mesh, in_specs=in_specs, out_specs=out_specs, check_vma=False)
```

```python
import jax
import jax.numpy as jnp
from jax import lax
from jax.experimental import pallas as pl
from jax.experimental.pallas import tpu as pltpu
from jax.sharding import PartitionSpec as P

EPS = 1e-06
CORES = 2
SLAB = 256


def along(array, count, target):
    return lax.ppermute(array, "expert", [(i, target(i)) for i in range(count)])


def ring(count, steps):
    return lambda i: (i + CORES * steps) % count


def next_layer(array, target):
    layers, count = lax.axis_size("section"), lax.axis_size("expert")
    route = [
        (layer * count + i, (layer + 1) * count + target(i))
        for layer in range(layers - 1)
        for i in range(count)
    ]
    return lax.ppermute(array, ("section", "expert"), route)


def against(matrix, activations):
    return lax.dot_general(
        matrix, activations, (((1,), (1,)), ((), ())), preferred_element_type=jnp.float32
    )


def silu_mix(gate, up):
    return gate / (1.0 + jnp.exp(-gate)) * up


def merge(is_upper, blend, own, other):
    of_own = jnp.where(is_upper, 1.0 - blend, blend)
    of_other = jnp.where(is_upper, blend, 1.0 - blend)
    return (of_own * own.astype(jnp.float32) + of_other * other.astype(jnp.float32)).astype(jnp.bfloat16)


def split_kernel(upper, projection, kept_in, kept_down, sent_in, sent_down):
    units = kept_down.shape[0]
    part = pl.program_id(0)
    turned = projection[0].T

    def put(kept, sent, at):
        @pl.when(upper[0] == 1)
        def _():
            kept[at, :] = turned[units:]
            sent[at, :] = turned[:units]

        @pl.when(upper[0] == 0)
        def _():
            kept[at, :] = turned[:units]
            sent[at, :] = turned[units:]

    for matrix in range(2):

        @pl.when(part == matrix)
        def _(matrix=matrix):
            put(kept_in, sent_in, pl.ds(matrix * units, units))

    @pl.when(part == 2)
    def _():
        put(kept_down, sent_down, pl.ds(0, units))


def blend_kernel(upper, members, x, own, other, merged, blend_out, sums, count):
    step = pl.program_id(0)
    units = sums.shape[1]
    lanes = sums.shape[2]

    @pl.when(step == 0)
    def _():
        sums[...] = jnp.zeros_like(sums)
        count[...] = jnp.zeros_like(count)

    def fold(array):
        return sum(array[:, i : i + lanes] for i in range(0, array.shape[1], lanes))

    for start in range(0, x.shape[0], SLAB):
        slab = pl.ds(start, SLAB)
        chosen = members[0][:, start : start + SLAB]
        hidden = []
        for weights in (own, other):
            out = against(weights[...], x[slab, :])
            hidden.append(silu_mix(out[:units], out[units:]).astype(jnp.bfloat16).astype(jnp.float32))
        mine, theirs = hidden
        weighted = chosen * mine
        sums[0] += fold(weighted * mine)
        sums[1] += fold(chosen * theirs * theirs)
        sums[2] += fold(weighted * theirs)
        count[...] += fold(chosen)

    @pl.when(step == pl.num_programs(0) - 1)
    def _():
        is_upper = upper[0] == 1
        used = jnp.maximum(jnp.sum(count[...], axis=1, keepdims=True), 1.0)
        energy_own, energy_other, cross_term = (
            jnp.sum(sums[i], axis=1, keepdims=True) / used for i in range(3)
        )
        energy_low = jnp.where(is_upper, energy_other, energy_own)
        energy_high = jnp.where(is_upper, energy_own, energy_other)
        agreement = 0.5 * (1.0 + cross_term / jnp.sqrt(energy_low * energy_high + EPS))
        root_low = jnp.sqrt(energy_low + EPS)
        root_high = jnp.sqrt(energy_high + EPS)
        blend = root_low / (root_low + agreement * root_high)
        blend_out[...] = jnp.broadcast_to(blend, blend_out.shape)
        for part in range(2):
            at = pl.ds(part * units, units)
            merged[at, :] = merge(is_upper, blend, own[at, :], other[at, :])


def weighted_terms(gate, up, down, x, weights, outs):
    units = gate.shape[0] // 2
    hidden = jnp.concatenate([ref[...] for ref in x], axis=0)
    hidden = silu_mix(against(gate[...], hidden), against(up[...], hidden))
    weight = jnp.concatenate([ref[0] for ref in weights], axis=1)
    inner = jnp.concatenate([hidden[:units] * weight[:1], hidden[units:] * weight[1:]], axis=0)
    out = lax.dot_general(
        inner.astype(jnp.bfloat16), down[...], (((0,), (0,)), ((), ())), preferred_element_type=jnp.float32
    ).astype(jnp.bfloat16)
    start = 0
    for ref in outs:
        ref[...] = out[start : start + ref.shape[0]]
        start += ref.shape[0]


def first_kernel(
    places, upper, weight_a, weight_b, weight_c, weight_d, x_a, x_b, x_c, x_d, merged_in, own_down, other_down,
    next_own, next_other, next_own_down, next_down, blend, next_blend, term_a, term_b, term_c, term_d, term_e, gate, up, down
):
    units = blend.shape[0]
    is_upper = upper[0] == 1
    mine = blend[:, :1]
    theirs = next_blend[:, :1]
    gate[:units] = merged_in[:units]
    up[:units] = merged_in[units:]
    down[:units] = merge(is_upper, mine, own_down[...], other_down[...])
    gate[units:] = merge(is_upper, theirs, next_own[:units], next_other[:units])
    up[units:] = merge(is_upper, theirs, next_own[units:], next_other[units:])
    down[units:] = merge(is_upper, theirs, next_own_down[...], next_down[...])
    weighted_terms(gate, up, down, (x_a, x_b), (weight_a, weight_b), (term_a, term_b, term_c))
    weighted_terms(gate, up, down, (x_c, x_d), (weight_c, weight_d), (term_d, term_e))


def terms_kernel(places, weight_a, weight_b, x_a, x_b, gate, up, down, *outs):
    for step in range(len(outs) // 2):

        @pl.when(pl.program_id(0) == step)
        def _(step=step):
            weighted_terms(gate, up, down, (x_a, x_b), (weight_a, weight_b), outs[2 * step : 2 * step + 2])


def local(tokens, routes, route_weight, projections):
    x_local = tokens[0]
    layer_routes = routes[0]
    layer_weight = route_weight[0]
    count = lax.axis_size("expert")
    pair_count = count // 2
    chips = count // CORES
    me = lax.axis_index("expert")
    chip, core = me // CORES, me % CORES
    is_upper = me >= pair_count
    upper = is_upper.astype(jnp.int32)[None]
    matrices, features, full_units = projections.shape[2:]
    units = full_units // 2
    rows = x_local.shape[0]
    across = lambda i: (i + pair_count) % count
    sibling = lambda i: i ^ 1

    x_all = lax.all_gather(x_local, "expert", axis=0, tiled=True)
    half_spec = lambda parts: pl.BlockSpec((parts * units, features), lambda i, *_: (0, 0))
    half = lambda parts: jax.ShapeDtypeStruct((parts * units, features), jnp.bfloat16)
    mine_in, mine_down, send_in, send_down = pl.pallas_call(
        split_kernel,
        grid_spec=pltpu.PrefetchScalarGridSpec(
            num_scalar_prefetch=1,
            grid=(matrices,),
            in_specs=[pl.BlockSpec((1, features, full_units), lambda i, *_: (i, 0, 0))],
            out_specs=[half_spec(2), half_spec(1), half_spec(2), half_spec(1)],
        ),
        out_shape=[half(2), half(1), half(2), half(1)],
        compiler_params=pltpu.CompilerParams(vmem_limit_bytes=32 << 20),
        cost_estimate=pl.CostEstimate(flops=0, bytes_accessed=4 * matrices * features * full_units, transcendentals=0),
        name="split",
    )(upper, projections[0, 0])
    partner_in = along(send_in, count, across)
    send_down, partner_in = lax.optimization_barrier((send_down, partner_in))
    partner_down = along(send_down, count, across)
    members, row_weight = [], []
    for pair in (me % pair_count, (me % pair_count) ^ 1):
        named = (layer_routes == pair) | (layer_routes == pair + pair_count)
        members.append(jnp.sum(named.astype(jnp.float32), axis=1))
        row_weight.append(jnp.sum(jnp.where(named, layer_weight, jnp.float32(0.0)), axis=1))
    row_weight = jnp.stack([array.reshape(count, rows) for array in row_weight], axis=1)
    far = chips // 2
    order = [far, far - 1, far + 1, 0, *(s for k in range(far - 2, 0, -1) for s in (k, chips - k))]
    places = ((chip + jnp.array(order, jnp.int32)) % chips) * CORES + core
    member, row_weight, first_places, places, kept_in, kept_down = lax.optimization_barrier(
        (members[0].reshape(-1, 1, 4 * rows), row_weight, places[:4], places[4:], mine_in, mine_down)
    )
    next_own = along(kept_in, count, sibling)
    next_own_down = along(kept_down, count, sibling)
    next_own, next_own_down, swapped = lax.optimization_barrier((next_own, next_own_down, partner_in))
    next_other = along(swapped, count, sibling)

    whole = lambda shape: pl.BlockSpec(shape, lambda i, *_: (0,) * len(shape))
    held = pl.BlockSpec(memory_space=pltpu.VMEM)
    total = x_all.shape[0]
    group = 4 * rows
    merged_in, blend = pl.pallas_call(
        blend_kernel,
        grid_spec=pltpu.PrefetchScalarGridSpec(
            num_scalar_prefetch=1,
            grid=(total // group,),
            in_specs=[
                pl.BlockSpec((1, 1, group), lambda i, *_: (i, 0, 0)),
                pl.BlockSpec((group, features), lambda i, *_: (i, 0)),
                whole((2 * units, features)),
                whole((2 * units, features)),
            ],
            out_specs=[whole((2 * units, features)), whole((units, 128))],
            scratch_shapes=[pltpu.VMEM((3, units, 128), jnp.float32), pltpu.VMEM((1, 128), jnp.float32)],
        ),
        out_shape=[
            jax.ShapeDtypeStruct((2 * units, features), jnp.bfloat16),
            jax.ShapeDtypeStruct((units, 128), jnp.float32),
        ],
        compiler_params=pltpu.CompilerParams(vmem_limit_bytes=32 << 20),
        cost_estimate=pl.CostEstimate(flops=8 * total * units * features, bytes_accessed=2 * total * features, transcendentals=0),
        name="blend",
    )(upper, member, x_all, mine_in, partner_in)
    next_blend = along(blend, count, sibling)
    partner_down, blend = lax.optimization_barrier((partner_down, blend))
    next_down = along(partner_down, count, sibling)

    weight_spec = lambda k: pl.BlockSpec((1, CORES, rows), lambda i, place, *_: (place[2 * i + k], 0, 0))
    x_spec = lambda k: pl.BlockSpec((rows, features), lambda i, place, *_: (place[2 * i + k], 0))
    blocks_in = lambda number: [weight_spec(k) for k in range(number)] + [x_spec(k) for k in range(number)]
    both = (2 * units, features)
    block = jax.ShapeDtypeStruct((rows, features), jnp.bfloat16)
    part = jax.ShapeDtypeStruct((rows // 2, features), jnp.bfloat16)
    low_rows, high_rows, *firsts, gate, up, down = pl.pallas_call(
        first_kernel,
        grid_spec=pltpu.PrefetchScalarGridSpec(
            num_scalar_prefetch=2,
            grid=(1,),
            in_specs=[
                *blocks_in(4),
                *[held] * 9,
            ],
            out_specs=[whole(part.shape)] * 2 + [whole(block.shape)] * 3 + [whole(both)] * 3,
        ),
        out_shape=[part] * 2 + [block] * 3 + [jax.ShapeDtypeStruct(both, jnp.bfloat16)] * 3,
        compiler_params=pltpu.CompilerParams(vmem_limit_bytes=40 << 20),
        cost_estimate=pl.CostEstimate(flops=24 * rows * units * features, bytes_accessed=20 * units * features, transcendentals=0),
        name="first",
    )(first_places, upper, *[row_weight] * 4, *[x_all] * 4, merged_in, mine_down, partner_down,
      next_own, next_other, next_own_down, next_down, blend, next_blend)
    others = pl.pallas_call(
        terms_kernel,
        grid_spec=pltpu.PrefetchScalarGridSpec(
            num_scalar_prefetch=1,
            grid=(chips // 2 - 2,),
            in_specs=[*blocks_in(2), whole(both), whole(both), whole(both)],
            out_specs=[whole(block.shape)] * (chips - 4),
        ),
        out_shape=[block] * (chips - 4),
        compiler_params=pltpu.CompilerParams(vmem_limit_bytes=40 << 20),
        cost_estimate=pl.CostEstimate(flops=24 * rows * units * features, bytes_accessed=4 * chips * rows * features, transcendentals=0),
        name="terms",
    )(places, row_weight, row_weight, x_all, x_all, gate, up, down)
    terms = dict(zip(order[1:], [*firsts, *others]))

    def add(*parts):
        return sum(part.astype(jnp.float32) for part in parts).astype(jnp.bfloat16)

    half = rows // 2
    behind, ahead = along(low_rows, count, ring(count, 1)), along(high_rows, count, ring(count, -1))
    three, minus_three = terms[far - 1], terms[chips - far + 1]
    grown = jnp.concatenate([add(behind, three[:half]), three[half:]], axis=0)
    minus_grown = jnp.concatenate([minus_three[:half], add(ahead, minus_three[half:])], axis=0)
    one = terms[1]
    grown, minus_grown, minus_one = lax.optimization_barrier((grown, minus_grown, terms[chips - 1]))
    grown = add(along(grown, count, ring(count, 1)), terms[far - 2])
    minus_grown = add(along(minus_grown, count, ring(count, -1)), terms[chips - far + 2])
    here = add(x_local, terms[0], along(one, count, ring(count, 1)), along(minus_one, count, ring(count, -1)))
    handed = add(
        next_layer(grown, ring(count, far - 2)),
        next_layer(minus_grown, ring(count, 2 - far)),
        next_layer(here, lambda i: i),
    )
    own = jnp.stack([gate[:units], up[:units], down[:units]])
    return (jnp.swapaxes(own, 1, 2)[None, None], handed[None])


def solution(mesh):
    in_specs = (
        P("section", "expert", None),
        P("section", None, None),
        P("section", None, None),
        P("section", "expert", None, None, None),
    )
    out_specs = (P("section", "expert", None, None, None), P("section", "expert", None))
    return jax.shard_map(local, mesh=mesh, in_specs=in_specs, out_specs=out_specs, check_vma=False)
```

```python
import jax
import jax.numpy as jnp
from jax import lax
from jax.experimental import pallas as pl
from jax.experimental.pallas import tpu as pltpu
from jax.sharding import PartitionSpec as P

EPS = 1e-06
CORES = 2
SLAB = 256


def along(array, count, target):
    return lax.ppermute(array, "expert", [(i, target(i)) for i in range(count)])


def ring(count, steps):
    return lambda i: (i + CORES * steps) % count


def next_layer(array, target):
    layers, count = lax.axis_size("section"), lax.axis_size("expert")
    route = [
        (layer * count + i, (layer + 1) * count + target(i))
        for layer in range(layers - 1)
        for i in range(count)
    ]
    return lax.ppermute(array, ("section", "expert"), route)


def against(matrix, activations):
    return lax.dot_general(
        matrix, activations, (((1,), (1,)), ((), ())), preferred_element_type=jnp.float32
    )


def silu_mix(gate, up):
    return gate / (1.0 + jnp.exp(-gate)) * up


def merge(is_upper, blend, own, other):
    of_own = jnp.where(is_upper, 1.0 - blend, blend)
    of_other = jnp.where(is_upper, blend, 1.0 - blend)
    return (of_own * own.astype(jnp.float32) + of_other * other.astype(jnp.float32)).astype(jnp.bfloat16)


def split_kernel(upper, projection, kept_in, kept_down, sent_in, sent_down):
    units = kept_down.shape[0]
    part = pl.program_id(0)
    turned = projection[0].T

    def put(kept, sent, at):
        @pl.when(upper[0] == 1)
        def _():
            kept[at, :] = turned[units:]
            sent[at, :] = turned[:units]

        @pl.when(upper[0] == 0)
        def _():
            kept[at, :] = turned[:units]
            sent[at, :] = turned[units:]

    for matrix in range(2):

        @pl.when(part == matrix)
        def _(matrix=matrix):
            put(kept_in, sent_in, pl.ds(matrix * units, units))

    @pl.when(part == 2)
    def _():
        put(kept_down, sent_down, pl.ds(0, units))


def blend_kernel(upper, members, x, own, other, merged, blend_out, parts_out, sums, count):
    step = pl.program_id(0)
    units = sums.shape[1]
    lanes = sums.shape[2]

    @pl.when(step == 0)
    def _():
        sums[...] = jnp.zeros_like(sums)
        count[...] = jnp.zeros_like(count)

    def fold(array):
        return sum(array[:, i : i + lanes] for i in range(0, array.shape[1], lanes))

    for start in range(0, x.shape[0], SLAB):
        slab = pl.ds(start, SLAB)
        chosen = members[0][:, start : start + SLAB]
        hidden = []
        for weights in (own, other):
            out = against(weights[...], x[slab, :])
            hidden.append(silu_mix(out[:units], out[units:]).astype(jnp.bfloat16).astype(jnp.float32))
        mine, theirs = hidden
        weighted = chosen * mine
        sums[0] += fold(weighted * mine)
        sums[1] += fold(chosen * theirs * theirs)
        sums[2] += fold(weighted * theirs)
        count[...] += fold(chosen)

    @pl.when(step == pl.num_programs(0) - 1)
    def _():
        is_upper = upper[0] == 1
        used = jnp.maximum(jnp.sum(count[...], axis=1, keepdims=True), 1.0)
        energy_own, energy_other, cross_term = (
            jnp.sum(sums[i], axis=1, keepdims=True) / used for i in range(3)
        )
        energy_low = jnp.where(is_upper, energy_other, energy_own)
        energy_high = jnp.where(is_upper, energy_own, energy_other)
        agreement = 0.5 * (1.0 + cross_term / jnp.sqrt(energy_low * energy_high + EPS))
        root_low = jnp.sqrt(energy_low + EPS)
        root_high = jnp.sqrt(energy_high + EPS)
        blend = root_low / (root_low + agreement * root_high)
        blend_out[...] = jnp.broadcast_to(blend, blend_out.shape)
        high = blend.astype(jnp.bfloat16)
        low = (blend - high.astype(jnp.float32)).astype(jnp.bfloat16)
        parts_out[:, :lanes] = jnp.broadcast_to(high, blend_out.shape)
        parts_out[:, lanes:] = jnp.broadcast_to(low, blend_out.shape)
        for part in range(2):
            at = pl.ds(part * units, units)
            merged[at, :] = merge(is_upper, blend, own[at, :], other[at, :])


def weighted_terms(gate, up, down, x, weights, outs):
    units = gate.shape[0] // 2
    hidden = jnp.concatenate([ref[...] for ref in x], axis=0)
    hidden = silu_mix(against(gate[...], hidden), against(up[...], hidden))
    weight = jnp.concatenate([ref[0] for ref in weights], axis=1)
    inner = jnp.concatenate([hidden[:units] * weight[:1], hidden[units:] * weight[1:]], axis=0)
    out = lax.dot_general(
        inner.astype(jnp.bfloat16), down[...], (((0,), (0,)), ((), ())), preferred_element_type=jnp.float32
    ).astype(jnp.bfloat16)
    start = 0
    for ref in outs:
        ref[...] = out[start : start + ref.shape[0]]
        start += ref.shape[0]


def first_kernel(
    places, upper, weight_a, weight_b, weight_c, weight_d, x_a, x_b, x_c, x_d, merged_in, own_down, other_down,
    next_own, next_other, next_own_down, next_down, blend, term_a, term_b, term_c, term_d, term_e, gate, up, down
):
    units = blend.shape[0]
    is_upper = upper[0] == 1
    mine = blend[:, :1]
    features = own_down.shape[1]
    high, low = next_down[:, features : features + 1], next_down[:, features + 128 : features + 129]
    theirs = high.astype(jnp.float32) + low.astype(jnp.float32)
    gate[:units] = merged_in[:units]
    up[:units] = merged_in[units:]
    down[:units] = merge(is_upper, mine, own_down[...], other_down[...])
    gate[units:] = merge(is_upper, theirs, next_own[:units], next_other[:units])
    up[units:] = merge(is_upper, theirs, next_own[units:], next_other[units:])
    down[units:] = merge(is_upper, theirs, next_own_down[...], next_down[:, :features])
    weighted_terms(gate, up, down, (x_a, x_b), (weight_a, weight_b), (term_a, term_b, term_c))
    weighted_terms(gate, up, down, (x_c, x_d), (weight_c, weight_d), (term_d, term_e))


def terms_kernel(places, weight_a, weight_b, x_a, x_b, gate, up, down, *outs):
    for step in range(len(outs) // 2):

        @pl.when(pl.program_id(0) == step)
        def _(step=step):
            weighted_terms(gate, up, down, (x_a, x_b), (weight_a, weight_b), outs[2 * step : 2 * step + 2])


def local(tokens, routes, route_weight, projections):
    x_local = tokens[0]
    layer_routes = routes[0]
    layer_weight = route_weight[0]
    count = lax.axis_size("expert")
    pair_count = count // 2
    chips = count // CORES
    me = lax.axis_index("expert")
    chip, core = me // CORES, me % CORES
    is_upper = me >= pair_count
    upper = is_upper.astype(jnp.int32)[None]
    matrices, features, full_units = projections.shape[2:]
    units = full_units // 2
    rows = x_local.shape[0]
    across = lambda i: (i + pair_count) % count
    sibling = lambda i: i ^ 1

    x_all = lax.all_gather(x_local, "expert", axis=0, tiled=True)
    half_spec = lambda parts: pl.BlockSpec((parts * units, features), lambda i, *_: (0, 0))
    half = lambda parts: jax.ShapeDtypeStruct((parts * units, features), jnp.bfloat16)
    mine_in, mine_down, send_in, send_down = pl.pallas_call(
        split_kernel,
        grid_spec=pltpu.PrefetchScalarGridSpec(
            num_scalar_prefetch=1,
            grid=(matrices,),
            in_specs=[pl.BlockSpec((1, features, full_units), lambda i, *_: (i, 0, 0))],
            out_specs=[half_spec(2), half_spec(1), half_spec(2), half_spec(1)],
        ),
        out_shape=[half(2), half(1), half(2), half(1)],
        compiler_params=pltpu.CompilerParams(vmem_limit_bytes=32 << 20),
        cost_estimate=pl.CostEstimate(flops=0, bytes_accessed=4 * matrices * features * full_units, transcendentals=0),
        name="split",
    )(upper, projections[0, 0])
    partner_in = along(send_in, count, across)
    send_down, partner_in = lax.optimization_barrier((send_down, partner_in))
    partner_down = along(send_down, count, across)
    members, row_weight = [], []
    for pair in (me % pair_count, (me % pair_count) ^ 1):
        named = (layer_routes == pair) | (layer_routes == pair + pair_count)
        members.append(jnp.sum(named.astype(jnp.float32), axis=1))
        row_weight.append(jnp.sum(jnp.where(named, layer_weight, jnp.float32(0.0)), axis=1))
    row_weight = jnp.stack([array.reshape(count, rows) for array in row_weight], axis=1)
    far = chips // 2
    order = [far, far - 1, far + 1, 0, *(s for k in range(far - 2, 0, -1) for s in (k, chips - k))]
    places = ((chip + jnp.array(order, jnp.int32)) % chips) * CORES + core
    member, row_weight, first_places, places, kept_in, kept_down = lax.optimization_barrier(
        (members[0].reshape(-1, 1, 4 * rows), row_weight, places[:4], places[4:], mine_in, mine_down)
    )
    next_own = along(kept_in, count, sibling)
    next_own_down = along(kept_down, count, sibling)
    next_own, next_own_down, swapped = lax.optimization_barrier((next_own, next_own_down, partner_in))
    next_other = along(swapped, count, sibling)

    whole = lambda shape: pl.BlockSpec(shape, lambda i, *_: (0,) * len(shape))
    held = pl.BlockSpec(memory_space=pltpu.VMEM)
    total = x_all.shape[0]
    group = 4 * rows
    merged_in, blend, blend_parts = pl.pallas_call(
        blend_kernel,
        grid_spec=pltpu.PrefetchScalarGridSpec(
            num_scalar_prefetch=1,
            grid=(total // group,),
            in_specs=[
                pl.BlockSpec((1, 1, group), lambda i, *_: (i, 0, 0)),
                pl.BlockSpec((group, features), lambda i, *_: (i, 0)),
                whole((2 * units, features)),
                whole((2 * units, features)),
            ],
            out_specs=[whole((2 * units, features)), whole((units, 128)), whole((units, 256))],
            scratch_shapes=[pltpu.VMEM((3, units, 128), jnp.float32), pltpu.VMEM((1, 128), jnp.float32)],
        ),
        out_shape=[
            jax.ShapeDtypeStruct((2 * units, features), jnp.bfloat16),
            jax.ShapeDtypeStruct((units, 128), jnp.float32),
            jax.ShapeDtypeStruct((units, 256), jnp.bfloat16),
        ],
        compiler_params=pltpu.CompilerParams(vmem_limit_bytes=32 << 20),
        cost_estimate=pl.CostEstimate(flops=8 * total * units * features, bytes_accessed=2 * total * features, transcendentals=0),
        name="blend",
    )(upper, member, x_all, mine_in, partner_in)
    next_down = along(jnp.concatenate([partner_down, blend_parts], axis=1), count, sibling)
    weight_spec = lambda k: pl.BlockSpec((1, CORES, rows), lambda i, place, *_: (place[2 * i + k], 0, 0))
    x_spec = lambda k: pl.BlockSpec((rows, features), lambda i, place, *_: (place[2 * i + k], 0))
    blocks_in = lambda number: [weight_spec(k) for k in range(number)] + [x_spec(k) for k in range(number)]
    both = (2 * units, features)
    block = jax.ShapeDtypeStruct((rows, features), jnp.bfloat16)
    part = jax.ShapeDtypeStruct((rows // 2, features), jnp.bfloat16)
    low_rows, high_rows, *firsts, gate, up, down = pl.pallas_call(
        first_kernel,
        grid_spec=pltpu.PrefetchScalarGridSpec(
            num_scalar_prefetch=2,
            grid=(1,),
            in_specs=[
                *blocks_in(4),
                *[held] * 8,
            ],
            out_specs=[whole(part.shape)] * 2 + [whole(block.shape)] * 3 + [whole(both)] * 3,
        ),
        out_shape=[part] * 2 + [block] * 3 + [jax.ShapeDtypeStruct(both, jnp.bfloat16)] * 3,
        compiler_params=pltpu.CompilerParams(vmem_limit_bytes=40 << 20),
        cost_estimate=pl.CostEstimate(flops=24 * rows * units * features, bytes_accessed=20 * units * features, transcendentals=0),
        name="first",
    )(first_places, upper, *[row_weight] * 4, *[x_all] * 4, merged_in, mine_down, partner_down,
      next_own, next_other, next_own_down, next_down, blend)
    others = pl.pallas_call(
        terms_kernel,
        grid_spec=pltpu.PrefetchScalarGridSpec(
            num_scalar_prefetch=1,
            grid=(chips // 2 - 2,),
            in_specs=[*blocks_in(2), whole(both), whole(both), whole(both)],
            out_specs=[whole(block.shape)] * (chips - 4),
        ),
        out_shape=[block] * (chips - 4),
        compiler_params=pltpu.CompilerParams(vmem_limit_bytes=40 << 20),
        cost_estimate=pl.CostEstimate(flops=24 * rows * units * features, bytes_accessed=4 * chips * rows * features, transcendentals=0),
        name="terms",
    )(places, row_weight, row_weight, x_all, x_all, gate, up, down)
    terms = dict(zip(order[1:], [*firsts, *others]))

    def add(*parts):
        return sum(part.astype(jnp.float32) for part in parts).astype(jnp.bfloat16)

    half = rows // 2
    behind, ahead = along(low_rows, count, ring(count, 1)), along(high_rows, count, ring(count, -1))
    three, minus_three = terms[far - 1], terms[chips - far + 1]
    grown = jnp.concatenate([add(behind, three[:half]), three[half:]], axis=0)
    minus_grown = jnp.concatenate([minus_three[:half], add(ahead, minus_three[half:])], axis=0)
    one = terms[1]
    grown, minus_grown, minus_one = lax.optimization_barrier((grown, minus_grown, terms[chips - 1]))
    grown = add(along(grown, count, ring(count, 1)), terms[far - 2])
    minus_grown = add(along(minus_grown, count, ring(count, -1)), terms[chips - far + 2])
    here = add(x_local, terms[0], along(one, count, ring(count, 1)), along(minus_one, count, ring(count, -1)))
    handed = add(
        next_layer(grown, ring(count, far - 2)),
        next_layer(minus_grown, ring(count, 2 - far)),
        next_layer(here, lambda i: i),
    )
    own = jnp.stack([gate[:units], up[:units], down[:units]])
    return (jnp.swapaxes(own, 1, 2)[None, None], handed[None])


def solution(mesh):
    in_specs = (
        P("section", "expert", None),
        P("section", None, None),
        P("section", None, None),
        P("section", "expert", None, None, None),
    )
    out_specs = (P("section", "expert", None, None, None), P("section", "expert", None))
    return jax.shard_map(local, mesh=mesh, in_specs=in_specs, out_specs=out_specs, check_vma=False)
```
